256 devices in a mesh: dp: 32 (over y, z_lo, core), tensor: 8 (over x, z_hi).
Axes of the slice: x: 4, y: 4, z: 8 (z_hi: 2, z_lo: 4; z = z_hi * 4 + z_lo), core: 2. Of those that a mesh axis runs over, the one named last changes fastest.
Arguments:
- acts: bfloat16 [32, 256, 8192], P('dp', None, 'tensor'), may hold values from -6 to 6
- out_grads: bfloat16 [32, 256, 14336], P('dp'), may hold values from -24 to 24
- projector: bfloat16 [8192, 128], P('tensor')
- weight: bfloat16 [8192, 14336], P('tensor', 'dp')
- first_moment: float32 [128, 14336], P(None, 'dp')
- second_moment: float32 [128, 14336], P(None, 'dp'), as said below
Outputs:
- new_weight: float32 [8192, 14336], P('tensor', 'dp')
- new_first: float32 [128, 14336], P(None, 'dp')
- new_second: float32 [128, 14336], P(None, 'dp')
The draws below stay inside these ranges and needn't reach their ends.
Inputs may be any that keep to these rules, and one draw needn't show every extreme that they name: `second_moment`: positive.
All inputs are finite; a program needn't handle non-finite values.
Results may differ from the reference program's by a relative error of at most 0.0033.
Values sent between devices are 32-bit elements; how exact they have to be, the bound alone decides.
No kernel may reach another device: no remote copies, remote signals or barrier semaphores. Data moves between devices by JAX's collectives and lax.ppermute only.
A program may use at most 128 MiB of HBM per device.

```python
import jax
import jax.numpy as jnp
from jax import lax

M = 8192
RANK = 128
COLS = 14336
TOK = 256
STEP = 10
REPLICAS = 32


def draw_projector(key, part):
    key = jax.random.fold_in(key, 7)
    base = jax.random.normal(key, (M, RANK), jnp.float32)
    where = jnp.arange(RANK, dtype=jnp.float32) / (RANK - 1)
    scales = 1.0 + 2.0 * where
    return (base * scales[None, :] / jnp.sqrt(jnp.float32(M))).astype(jnp.bfloat16)


def draw_weight(key, part):
    key = jax.random.fold_in(key, 17)
    spread = 0.01 * jnp.sqrt(jnp.float32(RANK) / jnp.float32(M))
    values = jax.random.normal(key, (M, COLS), jnp.float32)
    return (values * spread).astype(jnp.bfloat16)


def draw_first_moment(key, part):
    key = jax.random.fold_in(key, 11)
    spread = 0.1 / jnp.sqrt(jnp.float32(RANK * COLS))
    values = jax.random.normal(key, (RANK, COLS), jnp.float32)
    return (values * spread).astype(jnp.float32)


def draw_second_moment(key, part):
    key = jax.random.fold_in(key, 13)
    base = 1.0 / jnp.float32(RANK * COLS)
    values = jnp.exp(jax.random.uniform(key, (RANK, COLS), jnp.float32, -9.2103, -4.6052))
    return (values * base).astype(jnp.float32)


def levels(own_key, extent, pieces, least, top_value):
    factor_of = 1.0
    for dim, shards_of in pieces:
        steps = jax.random.uniform(jax.random.fold_in(jax.random.fold_in(own_key, 6), dim), (shards_of,), jnp.float32, least / len(pieces), top_value / len(pieces))
        factor_of = factor_of * jnp.repeat(jnp.exp(steps), extent[dim] // shards_of).reshape((-1,) + (1,) * (len(extent) - 1 - dim))
    return factor_of


def scatter_about(own_key, dims, deviation, most, shards=(), kind=jnp.bfloat16):
    level = levels(own_key, dims, shards, -0.22, 0.18) if shards else 1.0
    array = jax.random.normal(own_key, dims, jnp.float32) * deviation * level
    return jnp.minimum(jnp.maximum(array, -most), most).astype(kind)


def setup_inputs(seed: int = 0) -> dict:
    splits = jax.random.split(jax.random.key(seed), 7)
    return {
        "acts": scatter_about(splits[0], (REPLICAS, TOK, M), 1.0, 6.0, ((0, 32), (2, 8))),
        "out_grads": scatter_about(splits[1], (REPLICAS, TOK, COLS), 4.0, 24.0, ((0, 32),)),
        "projector": draw_projector(jax.random.fold_in(splits[6], 71), 0),
        "weight": draw_weight(jax.random.fold_in(splits[6], 71), 0),
        "first_moment": draw_first_moment(jax.random.fold_in(splits[6], 71), 0),
        "second_moment": draw_second_moment(jax.random.fold_in(splits[6], 71), 0),
    }


def reference(acts, out_grads, projector, weight, first_moment, second_moment):
    total = TOK * REPLICAS

    def one(carry, pair):
        xs, ys = pair
        grad = (lax.dot_general(xs, ys, (((0,), (0,)), ((), ())), preferred_element_type=jnp.float32) / total).astype(jnp.bfloat16)
        return (carry + grad.astype(jnp.float32), None)
    summed, unused = lax.scan(one, jnp.zeros((M, COLS), jnp.float32), (acts, out_grads))
    projected = lax.dot_general(projector.astype(jnp.float32), summed, (((0,), (0,)), ((), ())), precision=lax.Precision.HIGHEST, preferred_element_type=jnp.float32)
    squares = jnp.sum(projected * projected)
    factor = jnp.minimum(jnp.float32(1.0), 1.0 / jnp.sqrt(squares + 1e-12))
    clipped = factor * projected
    new_first = 0.9 * first_moment + 0.1 * clipped
    new_second = 0.999 * second_moment + 0.001 * clipped * clipped
    fix_one = 1.0 - 0.9 ** STEP
    fix_two = 1.0 - 0.999 ** STEP
    direction = (new_first / fix_one / (jnp.sqrt(new_second / fix_two) + 1e-08)).astype(jnp.bfloat16)
    delta = jnp.dot(projector, direction, preferred_element_type=jnp.float32)
    new_weight = weight.astype(jnp.float32) - 0.04 * 0.25 * delta
    return (new_weight, new_first, new_second)
```

```python
import jax
import jax.numpy as jnp
from jax import lax
from jax.sharding import Mesh
from jax.sharding import PartitionSpec as P

STEP = 10
FINE = ("y", "zl", "c", "x", "zh")
SIZES = (4, 4, 2, 4, 2)
DP = ("y", "zl", "c")
TENSOR = ("x", "zh")


def swap(value, axis):
    return lax.ppermute(value, axis, [(0, 1), (1, 0)])


def per_device(acts, out_grads, projector, weight, first_moment, second_moment):
    tokens = acts.shape[1]
    total = tokens * 32
    rank = projector.shape[1]
    columns = out_grads.shape[2]
    mine_cols = first_moment.shape[1]
    pair_cols = 2 * mine_cols
    chips = columns // pair_cols
    core = lax.axis_index("c")

    y_part = lax.dot_general(
        projector, acts[0], (((0,), (1,)), ((), ())), preferred_element_type=jnp.float32
    )
    mine = rank // 8
    blocks = y_part.reshape(2, 4, mine, tokens).transpose(1, 0, 2, 3).reshape(8, mine, tokens)
    blocks = lax.all_to_all(blocks, TENSOR, 0, 0, tiled=True)
    y = jnp.sum(blocks, axis=0) / total
    half = mine // 2
    own = lax.dynamic_slice_in_dim(y, core * half, half, 0)
    other = lax.dynamic_slice_in_dim(y, (1 - core) * half, half, 0)
    y = jnp.concatenate([own, other], axis=0)
    high = y.astype(jnp.bfloat16)
    low = (y - high.astype(jnp.float32)).astype(jnp.bfloat16)
    both = jnp.concatenate([high, low], axis=0)
    out = jnp.dot(both, out_grads[0], preferred_element_type=jnp.float32)
    out = out[:mine] + out[mine:]
    part = out[:half] + swap(out[half:], "c")
    part = part.reshape(half, chips, pair_cols).transpose(1, 0, 2)
    part = lax.all_to_all(part, ("y", "zl"), 0, 0, tiled=True)
    done = jnp.sum(part, axis=0)
    squares = jnp.sum(done * done)
    left, right = done[:, :mine_cols], done[:, mine_cols:]
    keep = jnp.where(core == 0, left, right)
    give = jnp.where(core == 0, right, left)
    give = jnp.concatenate([give, jnp.broadcast_to(squares, (half, 512 - mine_cols))], axis=1)
    got = swap(give, "c")
    squares = squares + got[0, mine_cols]
    got = got[:, :mine_cols]
    ranks = jnp.where(core == 0, jnp.concatenate([keep, got]), jnp.concatenate([got, keep]))
    send = jnp.concatenate([ranks, jnp.broadcast_to(squares, (mine, 512 - mine_cols))], axis=1)
    send = jnp.broadcast_to(send[None], (4,) + send.shape)
    rows = lax.all_to_all(send, "x", 0, 0, tiled=True)
    squares = jnp.sum(rows[:, 0, mine_cols])
    rows = rows[:, :, :mine_cols].reshape(4 * mine, mine_cols)
    far = swap(rows, "zh")
    zh = lax.axis_index("zh")
    projected = jnp.where(zh == 0, jnp.concatenate([rows, far]), jnp.concatenate([far, rows]))
    spread = jnp.broadcast_to(squares, (32, 8, 128))
    spread = lax.all_to_all(spread, ("y", "zl", "zh"), 0, 0, tiled=True)
    squares = jnp.sum(spread[:, 0, 0])

    factor = jnp.minimum(jnp.float32(1.0), 1.0 / jnp.sqrt(squares + 1e-12))
    clipped = factor * projected
    new_first = 0.9 * first_moment + 0.1 * clipped
    new_second = 0.999 * second_moment + 0.001 * clipped * clipped
    fix_one = 1.0 - 0.9**STEP
    fix_two = 1.0 - 0.999**STEP
    direction = (new_first / fix_one / (jnp.sqrt(new_second / fix_two) + 1e-08)).astype(
        jnp.bfloat16
    )
    delta = jnp.dot(projector, direction, preferred_element_type=jnp.float32)
    new_weight = weight.astype(jnp.float32) - 0.04 * 0.25 * delta
    return (new_weight, new_first, new_second)


def solution(mesh):
    fine = Mesh(mesh.devices.reshape(SIZES), FINE)
    placed = (
        P(DP, None, TENSOR),
        P(DP, None, None),
        P(TENSOR, None),
        P(TENSOR, DP),
        P(None, DP),
        P(None, DP),
    )
    return jax.shard_map(
        per_device,
        mesh=fine,
        in_specs=placed,
        out_specs=(P(TENSOR, DP), P(None, DP), P(None, DP)),
        check_vma=False,
    )
```

```python
import functools

import jax
import jax.numpy as jnp
from jax import lax
from jax.experimental import pallas as pl
from jax.experimental.pallas import tpu as pltpu
from jax.sharding import Mesh
from jax.sharding import PartitionSpec as P

STEP = 10
FINE = ("y", "zl", "c", "x", "zh")
SIZES = (4, 4, 2, 4, 2)
DP = ("y", "zl", "c")
TENSOR = ("x", "zh")
VMEM = pl.BlockSpec(memory_space=pltpu.VMEM)
SMEM = pl.BlockSpec(memory_space=pltpu.SMEM)
LIMIT = 32 << 20


def swap(value, axis):
    return lax.ppermute(value, axis, [(0, 1), (1, 0)])


def in_vmem(value):
    return pltpu.with_memory_space_constraint(value, pltpu.VMEM)


def call(body, outs, flops=0, nbytes=1 << 20):
    single = not isinstance(outs, list)
    made = [pltpu.VMEM(s, t) for s, t in ([outs] if single else outs)]
    return functools.partial(
        pl.pallas_call,
        body,
        out_shape=made[0] if single else tuple(made),
        out_specs=VMEM if single else tuple(VMEM for _ in made),
        compiler_params=pltpu.CompilerParams(vmem_limit_bytes=LIMIT),
        cost_estimate=pl.CostEstimate(flops=flops, bytes_accessed=nbytes, transcendentals=0),
    )


def first_body(acts_ref, proj_ref, out_ref):
    y = jnp.dot(acts_ref[...], proj_ref[...], preferred_element_type=jnp.float32)
    y = y.T
    mine = out_ref.shape[1]
    for x in range(4):
        for zh in range(2):
            begin = (zh * 4 + x) * mine
            out_ref[x * 2 + zh] = y[begin : begin + mine]


def second_body(total, core_ref, blocks_ref, og_ref, keep_ref, give_ref):
    y = blocks_ref[0]
    for i in range(1, blocks_ref.shape[0]):
        y = y + blocks_ref[i]
    y = y / total
    half = y.shape[0] // 2
    low_half, high_half = y[:half], y[half:]
    is_first = core_ref[0] == 0
    y = jnp.concatenate(
        [
            jnp.where(is_first, low_half, high_half),
            jnp.where(is_first, high_half, low_half),
        ]
    )
    high = y.astype(jnp.bfloat16)
    low = (y - high.astype(jnp.float32)).astype(jnp.bfloat16)
    both = jnp.concatenate([high, low])
    chips, _, width = keep_ref.shape
    for i in range(chips):
        out = jnp.dot(
            both, og_ref[:, i * width : (i + 1) * width], preferred_element_type=jnp.float32
        )
        out = out[: 2 * half] + out[2 * half :]
        keep_ref[i] = out[:half]
        give_ref[i] = out[half:]


def add_body(a_ref, b_ref, out_ref):
    out_ref[...] = a_ref[...] + b_ref[...]


def reduce_body(cols, core_ref, parts_ref, keep_ref, give_ref):
    done = parts_ref[0]
    for i in range(1, parts_ref.shape[0]):
        done = done + parts_ref[i]
    squares = jnp.sum(jnp.sum(done * done, axis=0, keepdims=True), axis=1, keepdims=True)
    wide = keep_ref.shape[1]
    left = done[:, :wide]
    right = pltpu.roll(done, cols, 1)[:, :wide]
    is_first = core_ref[0] == 0
    lane = lax.broadcasted_iota(jnp.int32, left.shape, 1)
    keep_ref[...] = jnp.where(lane < cols, jnp.where(is_first, left, right), squares)
    give_ref[...] = jnp.where(lane < cols, jnp.where(is_first, right, left), squares)


def pair_body(cols, core_ref, keep_ref, got_ref, out_ref):
    keep, got = keep_ref[...], got_ref[...]
    is_first = core_ref[0] == 0
    rows = jnp.concatenate([jnp.where(is_first, keep, got), jnp.where(is_first, got, keep)])
    both = keep + got
    both = jnp.concatenate([both, both])
    lane = lax.broadcasted_iota(jnp.int32, rows.shape, 1)
    rows = jnp.where(lane < cols, rows, both)
    for i in range(out_ref.shape[0]):
        out_ref[i] = rows


def norm_body(rows_ref, out_ref):
    wide = rows_ref.shape[2]
    total = rows_ref[0, 0:1, wide - 1 : wide]
    for i in range(1, rows_ref.shape[0]):
        total = total + rows_ref[i, 0:1, wide - 1 : wide]
    line = jnp.broadcast_to(total, (1, out_ref.shape[2]))
    for i in range(out_ref.shape[0]):
        out_ref[i] = line


def last_body(
    chunk,
    squares_ref,
    rows_ref,
    first_ref,
    second_ref,
    proj_ref,
    weight_ref,
    new_weight_ref,
    new_first_ref,
    new_second_ref,
    turned_ref,
):
    step = pl.program_id(0)

    @pl.when(step == 0)
    def _():
        rows = jnp.concatenate([rows_ref[x * 2 + zh] for zh in range(2) for x in range(4)])
        turned_ref[...] = rows.T

    squares = squares_ref[0]
    for i in range(1, squares_ref.shape[0]):
        squares = squares + squares_ref[i]
    factor = jnp.minimum(jnp.float32(1.0), 1.0 / jnp.sqrt(squares + 1e-12))
    clipped = factor * turned_ref[pl.ds(pl.multiple_of(step * chunk, 16), chunk), :]
    new_first = 0.9 * first_ref[...] + 0.1 * clipped
    new_second = 0.999 * second_ref[...] + 0.001 * clipped * clipped
    new_first_ref[...] = new_first
    new_second_ref[...] = new_second
    fix_one = 1.0 - 0.9**STEP
    fix_two = 1.0 - 0.999**STEP
    direction = (new_first / fix_one / (jnp.sqrt(new_second / fix_two) + 1e-08)).astype(
        jnp.bfloat16
    )
    delta = lax.dot_general(
        direction, proj_ref[...], (((1,), (1,)), ((), ())), preferred_element_type=jnp.float32
    )
    new_weight_ref[...] = weight_ref[...].astype(jnp.float32) - 0.04 * 0.25 * delta


def per_device(acts, out_grads, projector, weight, first_moment, second_moment):
    tokens = acts.shape[1]
    total = tokens * 32
    rows, rank = projector.shape
    columns = out_grads.shape[2]
    cols = first_moment.shape[1]
    chips = columns // (2 * cols)
    mine = rank // 8
    half = mine // 2
    wide = 512
    f32 = jnp.float32
    core = lax.axis_index("c").reshape(1)

    blocks = call(first_body, ((8, mine, tokens), f32))(in_specs=[VMEM, VMEM])(acts[0], projector)
    blocks = lax.all_to_all(blocks, TENSOR, 0, 0, tiled=True)
    block = ((chips, half, 2 * cols), f32)
    keep, give = call(functools.partial(second_body, float(total)), [block, block])(
        in_specs=[SMEM, VMEM, VMEM]
    )(core, blocks, in_vmem(out_grads[0]))
    part = call(add_body, block)(in_specs=[VMEM, VMEM])(keep, swap(give, "c"))
    part = lax.all_to_all(part, ("y", "zl"), 0, 0, tiled=True)
    small = ((half, wide), f32)
    keep, give = call(functools.partial(reduce_body, cols), [small, small])(
        in_specs=[SMEM, VMEM]
    )(core, part)
    sent = call(functools.partial(pair_body, cols), ((8, mine, wide), f32))(
        in_specs=[SMEM, VMEM, VMEM]
    )(core, keep, swap(give, "c"))
    got = lax.all_to_all(sent, TENSOR, 0, 0, tiled=True)
    squares = call(norm_body, ((chips, 1, 128), f32))(in_specs=[VMEM])(got)
    squares = lax.all_to_all(squares, ("y", "zl"), 0, 0, tiled=True)

    steps = 4
    chunk = cols // steps
    whole = lambda *shape: pl.BlockSpec(shape, lambda i: (0,) * len(shape))
    piece = lambda width: pl.BlockSpec((chunk, width), lambda i: (i, 0))
    new_weight, new_first, new_second = pl.pallas_call(
        functools.partial(last_body, chunk),
        grid=(steps,),
        in_specs=[
            whole(chips, 1, 128),
            whole(8, mine, wide),
            piece(rank),
            piece(rank),
            whole(rows, rank),
            piece(rows),
        ],
        out_specs=(piece(rows), piece(rank), piece(rank)),
        out_shape=(
            jax.ShapeDtypeStruct((cols, rows), f32),
            jax.ShapeDtypeStruct((cols, rank), f32),
            jax.ShapeDtypeStruct((cols, rank), f32),
        ),
        scratch_shapes=[pltpu.VMEM((wide, rank), f32)],
        compiler_params=pltpu.CompilerParams(vmem_limit_bytes=LIMIT),
        cost_estimate=pl.CostEstimate(
            flops=2 * cols * rows * rank, bytes_accessed=4 << 20, transcendentals=0
        ),
    )(squares, got, first_moment.T, second_moment.T, projector, weight.T)
    return (new_weight.T, new_first.T, new_second.T)


def solution(mesh):
    fine = Mesh(mesh.devices.reshape(SIZES), FINE)
    placed = (
        P(DP, None, TENSOR),
        P(DP, None, None),
        P(TENSOR, None),
        P(TENSOR, DP),
        P(None, DP),
        P(None, DP),
    )
    return jax.shard_map(
        per_device,
        mesh=fine,
        in_specs=placed,
        out_specs=(P(TENSOR, DP), P(None, DP), P(None, DP)),
        check_vma=False,
    )
```

```python
import functools

import jax
import jax.numpy as jnp
from jax import lax
from jax.experimental import pallas as pl
from jax.experimental.pallas import tpu as pltpu
from jax.sharding import Mesh
from jax.sharding import PartitionSpec as P

STEP = 10
FINE = ("y", "zl", "c", "x", "zh")
SIZES = (4, 4, 2, 4, 2)
DP = ("y", "zl", "c")
TENSOR = ("x", "zh")
VMEM = pl.BlockSpec(memory_space=pltpu.VMEM)
SMEM = pl.BlockSpec(memory_space=pltpu.SMEM)
HBM = pl.BlockSpec(memory_space=pl.ANY)
LIMIT = 6 << 20
F32 = jnp.float32
BF16 = jnp.bfloat16


def swap(value, axis):
    return lax.ppermute(value, axis, [(0, 1), (1, 0)])


def trade(values, axis):
    out = [values[0]]
    for k in (1, 2, 3):
        out.append(lax.ppermute(values[k], axis, [(i, i ^ k) for i in range(4)]))
    return out


def in_hbm(value):
    return pltpu.with_memory_space_constraint(value, pltpu.HBM)


def run(body, outs, specs, args, scratch=(), flops=0, nbytes=1 << 20):
    single = not isinstance(outs, list)
    made = [
        pltpu.VMEM(*(s if isinstance(s[0], tuple) else (s, F32))) for s in ([outs] if single else outs)
    ]
    return pl.pallas_call(
        body,
        in_specs=specs,
        out_shape=made[0] if single else tuple(made),
        out_specs=VMEM if single else tuple(VMEM for _ in made),
        scratch_shapes=list(scratch),
        compiler_params=pltpu.CompilerParams(vmem_limit_bytes=LIMIT),
        cost_estimate=pl.CostEstimate(flops=flops, bytes_accessed=nbytes, transcendentals=0),
    )(*args)


def total_of(refs):
    total = refs[0][...]
    for ref in refs[1:]:
        total = total + ref[...]
    return total


def first_body(x_ref, acts_hbm, proj_hbm, *rest):
    outs, (acts_ref, proj_ref, turned_ref, sems) = rest[:-4], rest[-4:]
    one = pltpu.make_async_copy(acts_hbm, acts_ref, sems.at[0])
    two = pltpu.make_async_copy(proj_hbm, proj_ref, sems.at[1])
    two.start()
    one.start()
    two.wait()
    one.wait()
    y = jnp.dot(acts_ref[...], proj_ref[...], preferred_element_type=F32)
    turned_ref[...] = y.T
    for k in range(4):
        begin = pl.multiple_of((x_ref[0] ^ k) * 32, 32)
        outs[k][...] = turned_ref[pl.ds(begin, 32), :]


def fetch_body(og_hbm, after_ref, og_ref, sems):
    rows = og_hbm.shape[0] // sems.shape[0]
    copies = []
    for n in range(sems.shape[0]):
        part = pl.ds(n * rows, rows)
        copies.append(pltpu.make_async_copy(og_hbm.at[part], og_ref.at[part], sems.at[n]))
        copies[-1].start()
    for copy in copies:
        copy.wait()


def split_body(zh_ref, *refs):
    ins, (keep_ref, give_ref) = refs[:4], refs[4:]
    y = total_of(ins)
    low = jnp.concatenate([y[0:8], y[16:24]])
    high = jnp.concatenate([y[8:16], y[24:32]])
    is_first = zh_ref[0] == 0
    keep_ref[...] = jnp.where(is_first, low, high)
    give_ref[...] = jnp.where(is_first, high, low)


def second_body(total, c_ref, one_ref, two_ref, og_ref, keep_ref, give_ref):
    y = (one_ref[...] + two_ref[...]) / total
    low_half, high_half = y[:8], y[8:]
    is_first = c_ref[0] == 0
    y = jnp.concatenate(
        [
            jnp.where(is_first, low_half, high_half),
            jnp.where(is_first, high_half, low_half),
        ]
    )
    high = y.astype(BF16)
    low = (y - high.astype(F32)).astype(BF16)
    both = jnp.concatenate([high, low])
    chips, _, width = keep_ref.shape
    for i in range(chips):
        columns = og_ref[:, i * width : (i + 1) * width]
        out = jnp.dot(both, columns, preferred_element_type=F32)
        out = out[:16] + out[16:]
        keep_ref[i] = out[:8]
        give_ref[i] = out[8:]


def by_y_body(y_ref, a_ref, b_ref, *outs):
    for k in range(4):
        begin = (y_ref[0] ^ k) * 4
        outs[k][...] = a_ref[pl.ds(begin, 4)] + b_ref[pl.ds(begin, 4)]


def by_zl_body(zl_ref, *refs):
    ins, outs = refs[:4], refs[4:]
    for k in range(4):
        at = zl_ref[0] ^ k
        outs[k][...] = ins[0][at] + ins[1][at] + ins[2][at] + ins[3][at]


def squares_body(*refs):
    ins, (done_ref, line_ref) = refs[:-2], refs[-2:]
    done = total_of(ins)
    width = done.shape[1]
    squares = jnp.sum(jnp.sum(done * done, axis=0, keepdims=True), axis=1, keepdims=True)
    done_ref[:, :width] = done
    done_ref[:, width:] = jnp.broadcast_to(squares, done_ref[:, width:].shape)
    line_ref[...] = jnp.broadcast_to(squares, line_ref.shape)


def both_cores_body(done_ref, line_ref, out_ref):
    width = out_ref.shape[1] - 128
    out_ref[:, :width] = done_ref[:, :width]
    out_ref[:, width:] = done_ref[:, width:] + line_ref[0:1, :]


def by_column_body(cols, zh_ref, c_ref, keep_ref, got_ref, squares_ref, own_ref, give_ref):
    keep, got = keep_ref[...], got_ref[...]
    width = keep.shape[1] - 128
    is_first = zh_ref[0] == 0
    rows = jnp.concatenate([jnp.where(is_first, keep, got), jnp.where(is_first, got, keep)])
    squares_ref[...] = jnp.broadcast_to(
        keep[0:1, width:] + got[0:1, width:], squares_ref.shape
    )
    wide = own_ref.shape[1]
    left = rows[:, :wide]
    right = pltpu.roll(rows[:, :width], cols, 1)[:, :wide]
    is_first = c_ref[0] == 0
    own_ref[...] = jnp.where(is_first, left, right)
    give_ref[...] = jnp.where(is_first, right, left)


def by_core_body(c_ref, keep_ref, got_ref, out_ref):
    keep, got = keep_ref[...], got_ref[...]
    is_first = c_ref[0] == 0
    out_ref[:16] = jnp.where(is_first, keep, got)
    out_ref[16:] = jnp.where(is_first, got, keep)


def last_body(
    steps,
    x_ref,
    squares_ref,
    lines0_ref,
    lines1_ref,
    lines2_ref,
    lines3_ref,
    first_ref,
    second_ref,
    proj_ref,
    weight_ref,
    new_weight_hbm,
    new_first_hbm,
    new_second_hbm,
    rows_ref,
    turned_ref,
    new_weight_ref,
    new_first_ref,
    new_second_ref,
    sems,
):
    for k, ref in enumerate((lines0_ref, lines1_ref, lines2_ref, lines3_ref)):
        begin = pl.multiple_of((x_ref[0] ^ k) * 32, 32)
        rows_ref[pl.ds(begin, 32), :] = ref[...]
    turned_ref[...] = rows_ref[...].T
    squares = jnp.sum(squares_ref[...], axis=0)[0:1]
    factor = jnp.minimum(jnp.float32(1.0), 1.0 / jnp.sqrt(squares + 1e-12))
    fix_one = 1.0 - 0.9**STEP
    fix_two = 1.0 - 0.999**STEP
    chunk = first_ref.shape[0] // steps
    copies = []
    for i in range(steps):
        here = pl.ds(i * chunk, chunk)
        clipped = factor * turned_ref[here, :]
        new_first = 0.9 * first_ref[here, :] + 0.1 * clipped
        new_second = 0.999 * second_ref[here, :] + 0.001 * clipped * clipped
        new_first_ref[here, :] = new_first
        new_second_ref[here, :] = new_second
        direction = new_first / fix_one / (jnp.sqrt(new_second / fix_two) + 1e-08)
        delta = lax.dot_general(
            direction.astype(BF16),
            proj_ref[...],
            (((1,), (1,)), ((), ())),
            preferred_element_type=F32,
        )
        new_weight_ref[here, :] = weight_ref[here, :].astype(F32) - 0.04 * 0.25 * delta
        for n, (src, dst) in enumerate(
            (
                (new_weight_ref, new_weight_hbm),
                (new_first_ref, new_first_hbm),
                (new_second_ref, new_second_hbm),
            )
        ):
            copies.append(pltpu.make_async_copy(src.at[here], dst.at[here], sems.at[i, n]))
            copies[-1].start()
    for copy in copies:
        copy.wait()


def per_device(acts, out_grads, projector, weight, first_moment, second_moment):
    tokens = acts.shape[1]
    total = float(tokens * 32)
    rows, rank = projector.shape
    columns = out_grads.shape[2]
    cols = first_moment.shape[1]
    width = 2 * cols
    chips = columns // width
    wide = 512
    me_y, me_zl, me_c, me_x, me_zh = [lax.axis_index(name).reshape(1) for name in FINE]

    y = run(
        first_body,
        [(32, tokens)] * 4,
        [SMEM, HBM, HBM],
        (me_x, in_hbm(acts[0]), in_hbm(projector)),
        [
            pltpu.VMEM((tokens, rows), BF16),
            pltpu.VMEM((rows, rank), BF16),
            pltpu.VMEM((rank, tokens), F32),
            pltpu.SemaphoreType.DMA((2,)),
        ],
    )
    y = trade(y, "x")
    keep, give = run(split_body, [(16, tokens)] * 2, [SMEM] + [VMEM] * 4, (me_zh, *y))
    got = swap(give, "zh")
    og = run(
        fetch_body,
        ((tokens, columns), BF16),
        [HBM, HBM],
        (in_hbm(out_grads[0]), keep),
        [pltpu.SemaphoreType.DMA((4,))],
        nbytes=16 << 20,
    )
    keep, give = run(
        functools.partial(second_body, total),
        [(chips, 8, width)] * 2,
        [SMEM] + [VMEM] * 3,
        (me_c, keep, got, og),
        flops=2 * 32 * tokens * columns,
        nbytes=8 << 20,
    )
    parts = run(by_y_body, [(4, 8, width)] * 4, [SMEM, VMEM, VMEM], (me_y, keep, swap(give, "c")))
    parts = trade(parts, "y")
    parts = run(by_zl_body, [(8, width)] * 4, [SMEM] + [VMEM] * 4, (me_zl, *parts))
    parts = trade(parts, "zl")
    done, line = run(squares_body, [(8, width + 128), (8, 128)], [VMEM] * 4, tuple(parts))
    done = run(both_cores_body, (8, width + 128), [VMEM] * 2, (done, swap(line, "c")))
    squares, keep, give = run(
        functools.partial(by_column_body, cols),
        [(64, 2, 128), (16, wide), (16, wide)],
        [SMEM, SMEM, VMEM, VMEM],
        (me_zh, me_c, done, swap(done, "zh")),
    )
    squares = lax.all_to_all(squares, ("y", "zl", "x"), 0, 0, tiled=True)
    lines = run(by_core_body, (32, wide), [SMEM, VMEM, VMEM], (me_c, keep, swap(give, "c")))
    lines = trade([lines] * 4, "x")

    steps = 4
    outs = [(cols, rows), (cols, rank), (cols, rank)]
    new_weight, new_first, new_second = pl.pallas_call(
        functools.partial(last_body, steps),
        in_specs=[SMEM] + [VMEM] * 9,
        out_specs=(HBM,) * 3,
        out_shape=tuple(jax.ShapeDtypeStruct(shape, F32) for shape in outs),
        scratch_shapes=[
            pltpu.VMEM((rank, wide), F32),
            pltpu.VMEM((wide, rank), F32),
            *[pltpu.VMEM(shape, F32) for shape in outs],
            pltpu.SemaphoreType.DMA((steps, 3)),
        ],
        compiler_params=pltpu.CompilerParams(vmem_limit_bytes=LIMIT),
        cost_estimate=pl.CostEstimate(
            flops=2 * cols * rows * rank, bytes_accessed=4 << 20, transcendentals=0
        ),
    )(me_x, squares, *lines, first_moment.T, second_moment.T, projector, weight.T)
    return (new_weight.T, new_first.T, new_second.T)


def solution(mesh):
    fine = Mesh(mesh.devices.reshape(SIZES), FINE)
    placed = (
        P(DP, None, TENSOR),
        P(DP, None, None),
        P(TENSOR, None),
        P(TENSOR, DP),
        P(None, DP),
        P(None, DP),
    )
    return jax.shard_map(
        per_device,
        mesh=fine,
        in_specs=placed,
        out_specs=(P(TENSOR, DP), P(None, DP), P(None, DP)),
        check_vma=False,
    )
```

```python
import functools

import jax
import jax.numpy as jnp
from jax import lax
from jax.experimental import pallas as pl
from jax.experimental.pallas import tpu as pltpu
from jax.sharding import Mesh
from jax.sharding import PartitionSpec as P

STEP = 10
FINE = ("y", "zl", "c", "x", "zh")
SIZES = (4, 4, 2, 4, 2)
DP = ("y", "zl", "c")
TENSOR = ("x", "zh")
VMEM = pl.BlockSpec(memory_space=pltpu.VMEM)
SMEM = pl.BlockSpec(memory_space=pltpu.SMEM)
HBM = pl.BlockSpec(memory_space=pl.ANY)
LIMIT = 6 << 20
ORDER = (3, 2, 1, 0)
F32 = jnp.float32
BF16 = jnp.bfloat16


def swap(value, axis):
    return lax.ppermute(value, axis, [(0, 1), (1, 0)])


def trade(values, axis):
    return [lax.ppermute(values[k], axis, [(i, i ^ k) for i in range(4)]) for k in ORDER[:3]] + [
        values[0]
    ]


def in_hbm(value):
    return pltpu.with_memory_space_constraint(value, pltpu.HBM)


def run(body, outs, specs, args, scratch=(), flops=0, nbytes=1 << 20):
    single = not isinstance(outs, list)
    made = [
        pltpu.VMEM(*(s if isinstance(s[0], tuple) else (s, F32))) for s in ([outs] if single else outs)
    ]
    return pl.pallas_call(
        body,
        in_specs=specs,
        out_shape=made[0] if single else tuple(made),
        out_specs=VMEM if single else tuple(VMEM for _ in made),
        scratch_shapes=list(scratch),
        compiler_params=pltpu.CompilerParams(vmem_limit_bytes=LIMIT),
        cost_estimate=pl.CostEstimate(flops=flops, bytes_accessed=nbytes, transcendentals=0),
    )(*args)


def total_of(refs):
    total = refs[0][...]
    for ref in refs[1:]:
        total = total + ref[...]
    return total


def first_body(x_ref, acts_hbm, proj_hbm, *rest):
    outs, (acts_ref, proj_ref, turned_ref, sems) = rest[:-4], rest[-4:]
    one = pltpu.make_async_copy(acts_hbm, acts_ref, sems.at[0])
    two = pltpu.make_async_copy(proj_hbm, proj_ref, sems.at[1])
    two.start()
    one.start()
    two.wait()
    one.wait()
    y = jnp.dot(acts_ref[...], proj_ref[...], preferred_element_type=F32)
    turned_ref[...] = y.T
    for k in range(4):
        begin = pl.multiple_of((x_ref[0] ^ k) * 32, 32)
        outs[k][...] = turned_ref[pl.ds(begin, 32), :]


def fetch_body(og_hbm, after_ref, og_ref, sems):
    rows = og_hbm.shape[0] // sems.shape[0]
    copies = []
    for n in range(sems.shape[0]):
        part = pl.ds(n * rows, rows)
        copies.append(pltpu.make_async_copy(og_hbm.at[part], og_ref.at[part], sems.at[n]))
        copies[-1].start()
    for copy in copies:
        copy.wait()


def split_body(zh_ref, *refs):
    ins, (keep_ref, give_ref) = refs[:4], refs[4:]
    y = total_of(ins)
    low, high = y[:16], y[16:]
    is_first = zh_ref[0] == 0
    keep_ref[...] = jnp.where(is_first, low, high)
    give_ref[...] = jnp.where(is_first, high, low)


def second_body(total, c_ref, one_ref, two_ref, og_ref, keep_ref, give_ref):
    y = (one_ref[...] + two_ref[...]) / total
    low_half, high_half = y[:8], y[8:]
    is_first = c_ref[0] == 0
    y = jnp.concatenate(
        [
            jnp.where(is_first, low_half, high_half),
            jnp.where(is_first, high_half, low_half),
        ]
    )
    high = y.astype(BF16)
    low = (y - high.astype(F32)).astype(BF16)
    both = jnp.concatenate([high, low])
    chips, _, width = keep_ref.shape
    for i in range(chips):
        columns = og_ref[:, i * width : (i + 1) * width]
        out = jnp.dot(both, columns, preferred_element_type=F32)
        out = out[:16] + out[16:]
        keep_ref[i] = out[:8]
        give_ref[i] = out[8:]


def by_y_body(y_ref, a_ref, b_ref, *outs):
    for k in range(4):
        begin = (y_ref[0] ^ k) * 4
        outs[k][...] = a_ref[pl.ds(begin, 4)] + b_ref[pl.ds(begin, 4)]


def by_zl_body(zl_ref, *refs):
    ins, outs = refs[:4], refs[4:]
    for k in range(4):
        at = zl_ref[0] ^ k
        outs[k][...] = ins[0][at] + ins[1][at] + ins[2][at] + ins[3][at]


def reduce_body(cols, c_ref, *refs):
    ins, (keep_ref, give_ref) = refs[:-2], refs[-2:]
    if len(ins) == 1:
        parts_ref = ins[0]
        done = []
        for zh in range(2):
            plane = parts_ref[4 * zh]
            for zl in range(1, 4):
                plane = plane + parts_ref[4 * zh + zl]
            done.append(plane)
        done = jnp.concatenate(done)
    else:
        done = total_of(ins)
    squares = jnp.sum(jnp.sum(done * done, axis=0, keepdims=True), axis=1, keepdims=True)
    wide = keep_ref.shape[1]
    left = done[:, :wide]
    right = pltpu.roll(done, cols, 1)[:, :wide]
    is_first = c_ref[0] == 0
    lane = lax.broadcasted_iota(jnp.int32, left.shape, 1)
    keep_ref[...] = jnp.where(lane < cols, jnp.where(is_first, left, right), squares)
    give_ref[...] = jnp.where(lane < cols, jnp.where(is_first, right, left), squares)


def pair_body(cols, me_ref, keep_ref, got_ref, *outs):
    keep, got = keep_ref[...], got_ref[...]
    is_first = me_ref[0] == 0
    half = keep.shape[0]
    both = keep + got
    lane = lax.broadcasted_iota(jnp.int32, keep.shape, 1)
    outs[0][:half] = jnp.where(lane < cols, jnp.where(is_first, keep, got), both)
    outs[0][half:] = jnp.where(lane < cols, jnp.where(is_first, got, keep), both)
    if len(outs) == 2:
        line = both[0:1, both.shape[1] - 1 :]
        outs[1][...] = jnp.broadcast_to(line, outs[1].shape)


def last_body(
    steps,
    x_ref,
    squares_ref,
    lines0_ref,
    lines1_ref,
    lines2_ref,
    lines3_ref,
    first_ref,
    second_ref,
    proj_ref,
    weight_ref,
    new_weight_hbm,
    new_first_hbm,
    new_second_hbm,
    rows_ref,
    turned_ref,
    new_weight_ref,
    new_first_ref,
    new_second_ref,
    sems,
):
    for k, ref in zip(ORDER, (lines0_ref, lines1_ref, lines2_ref, lines3_ref)):
        begin = pl.multiple_of((x_ref[0] ^ k) * 32, 32)
        rows_ref[pl.ds(begin, 32), :] = ref[...]
    turned_ref[...] = rows_ref[...].T
    squares = jnp.sum(squares_ref[...], axis=0)[0:1]
    factor = jnp.minimum(jnp.float32(1.0), 1.0 / jnp.sqrt(squares + 1e-12))
    fix_one = 1.0 - 0.9**STEP
    fix_two = 1.0 - 0.999**STEP
    chunk = first_ref.shape[0] // steps
    copies = []
    for i in range(steps):
        here = pl.ds(i * chunk, chunk)
        clipped = factor * turned_ref[here, :]
        new_first = 0.9 * first_ref[here, :] + 0.1 * clipped
        new_second = 0.999 * second_ref[here, :] + 0.001 * clipped * clipped
        new_first_ref[here, :] = new_first
        new_second_ref[here, :] = new_second
        direction = new_first / fix_one / (jnp.sqrt(new_second / fix_two) + 1e-08)
        delta = lax.dot_general(
            direction.astype(BF16),
            proj_ref[...],
            (((1,), (1,)), ((), ())),
            preferred_element_type=F32,
        )
        new_weight_ref[here, :] = weight_ref[here, :].astype(F32) - 0.04 * 0.25 * delta
        for n, (src, dst) in enumerate(
            (
                (new_weight_ref, new_weight_hbm),
                (new_first_ref, new_first_hbm),
                (new_second_ref, new_second_hbm),
            )
        ):
            copies.append(pltpu.make_async_copy(src.at[here], dst.at[here], sems.at[i, n]))
            copies[-1].start()
    for copy in copies:
        copy.wait()


def per_device(acts, out_grads, projector, weight, first_moment, second_moment):
    tokens = acts.shape[1]
    total = float(tokens * 32)
    rows, rank = projector.shape
    columns = out_grads.shape[2]
    cols = first_moment.shape[1]
    width = 2 * cols
    chips = columns // width
    wide = 512
    me_y, me_zl, me_c, me_x, me_zh = [lax.axis_index(name).reshape(1) for name in FINE]

    y = run(
        first_body,
        [(32, tokens)] * 4,
        [SMEM, HBM, HBM],
        (me_x, in_hbm(acts[0]), in_hbm(projector)),
        [
            pltpu.VMEM((tokens, rows), BF16),
            pltpu.VMEM((rows, rank), BF16),
            pltpu.VMEM((rank, tokens), F32),
            pltpu.SemaphoreType.DMA((2,)),
        ],
    )
    y = trade(y, "x")
    keep, give = run(split_body, [(16, tokens)] * 2, [SMEM] + [VMEM] * 4, (me_zh, *y))
    got = swap(give, "zh")
    og = run(
        fetch_body,
        ((tokens, columns), BF16),
        [HBM, HBM],
        (in_hbm(out_grads[0]), keep),
        [pltpu.SemaphoreType.DMA((4,))],
        nbytes=16 << 20,
    )
    keep, give = run(
        functools.partial(second_body, total),
        [(chips, 8, width)] * 2,
        [SMEM] + [VMEM] * 3,
        (me_c, keep, got, og),
        flops=2 * 32 * tokens * columns,
        nbytes=8 << 20,
    )
    parts = run(by_y_body, [(4, 8, width)] * 4, [SMEM, VMEM, VMEM], (me_y, keep, swap(give, "c")))
    parts = trade(parts, "y")
    parts = run(by_zl_body, [(8, width)] * 4, [SMEM] + [VMEM] * 4, (me_zl, *parts))
    parts = trade(parts, "zl")
    pair = functools.partial(pair_body, cols)
    keep, give = run(
        functools.partial(reduce_body, cols),
        [(8, wide)] * 2,
        [SMEM] + [VMEM] * 4,
        (me_c, *parts),
    )
    keep = run(pair, (16, wide), [SMEM, VMEM, VMEM], (me_c, keep, swap(give, "c")))
    line, squares = run(
        pair,
        [(32, wide), (64, 2, 128)],
        [SMEM, VMEM, VMEM],
        (me_zh, keep, swap(keep, "zh")),
    )
    squares = lax.all_to_all(squares, ("y", "zl", "x"), 0, 0, tiled=True)
    lines = trade([line] * 4, "x")

    steps = 4
    outs = [(cols, rows), (cols, rank), (cols, rank)]
    new_weight, new_first, new_second = pl.pallas_call(
        functools.partial(last_body, steps),
        in_specs=[SMEM] + [VMEM] * 9,
        out_specs=(HBM,) * 3,
        out_shape=tuple(jax.ShapeDtypeStruct(shape, F32) for shape in outs),
        scratch_shapes=[
            pltpu.VMEM((rank, wide), F32),
            pltpu.VMEM((wide, rank), F32),
            *[pltpu.VMEM(shape, F32) for shape in outs],
            pltpu.SemaphoreType.DMA((steps, 3)),
        ],
        compiler_params=pltpu.CompilerParams(vmem_limit_bytes=LIMIT),
        cost_estimate=pl.CostEstimate(
            flops=2 * cols * rows * rank, bytes_accessed=4 << 20, transcendentals=0
        ),
    )(me_x, squares, *lines, first_moment.T, second_moment.T, projector, weight.T)
    return (new_weight.T, new_first.T, new_second.T)


def solution(mesh):
    fine = Mesh(mesh.devices.reshape(SIZES), FINE)
    placed = (
        P(DP, None, TENSOR),
        P(DP, None, None),
        P(TENSOR, None),
        P(TENSOR, DP),
        P(None, DP),
        P(None, DP),
    )
    return jax.shard_map(
        per_device,
        mesh=fine,
        in_specs=placed,
        out_specs=(P(TENSOR, DP), P(None, DP), P(None, DP)),
        check_vma=False,
    )
```

```python
import functools

import jax
import jax.numpy as jnp
from jax import lax
from jax.experimental import pallas as pl
from jax.experimental.pallas import tpu as pltpu
from jax.sharding import Mesh
from jax.sharding import PartitionSpec as P

STEP = 10
FINE = ("y", "zl", "c", "x", "zh")
SIZES = (4, 4, 2, 4, 2)
DP = ("y", "zl", "c")
TENSOR = ("x", "zh")
VMEM = pl.BlockSpec(memory_space=pltpu.VMEM)
SMEM = pl.BlockSpec(memory_space=pltpu.SMEM)
HBM = pl.BlockSpec(memory_space=pl.ANY)
LIMIT = 6 << 20
ORDER = (3, 2, 1, 0)
F32 = jnp.float32
BF16 = jnp.bfloat16


def swap(value, axis):
    return lax.ppermute(value, axis, [(0, 1), (1, 0)])


def trade(values, axis, order=(3, 2, 1)):
    return [lax.ppermute(values[k], axis, [(i, i ^ k) for i in range(4)]) for k in order] + [
        values[0]
    ]


def in_hbm(value):
    return pltpu.with_memory_space_constraint(value, pltpu.HBM)


def run(body, outs, specs, args, scratch=(), flops=0, nbytes=1 << 20):
    single = not isinstance(outs, list)
    made = [
        pltpu.VMEM(*(s if isinstance(s[0], tuple) else (s, F32))) for s in ([outs] if single else outs)
    ]
    return pl.pallas_call(
        body,
        in_specs=specs,
        out_shape=made[0] if single else tuple(made),
        out_specs=VMEM if single else tuple(VMEM for _ in made),
        scratch_shapes=list(scratch),
        compiler_params=pltpu.CompilerParams(vmem_limit_bytes=LIMIT),
        cost_estimate=pl.CostEstimate(flops=flops, bytes_accessed=nbytes, transcendentals=0),
    )(*args)


def total_of(refs):
    total = refs[0][...]
    for ref in refs[1:]:
        total = total + ref[...]
    return total


def first_body(x_ref, acts_hbm, proj_hbm, *rest):
    outs, (acts_ref, proj_ref, turned_ref, sems) = rest[:-4], rest[-4:]
    half = acts_ref.shape[0] // 2
    whole = pltpu.make_async_copy(proj_hbm, proj_ref, sems.at[2])
    whole.start()
    copies = []
    for n in range(2):
        here = pl.ds(n * half, half)
        copies.append(pltpu.make_async_copy(acts_hbm.at[here], acts_ref.at[here], sems.at[n]))
        copies[-1].start()
    whole.wait()
    for n in range(2):
        copies[n].wait()
        y = jnp.dot(
            acts_ref[n * half : (n + 1) * half, :], proj_ref[...], preferred_element_type=F32
        )
        turned_ref[:, n * half : (n + 1) * half] = y.T
    for k in range(4):
        begin = pl.multiple_of((x_ref[0] ^ k) * 32, 32)
        outs[k][...] = turned_ref[pl.ds(begin, 32), :]


def fetch_body(og_hbm, after_ref, og_ref, sems):
    rows = og_hbm.shape[0] // sems.shape[0]
    copies = []
    for n in range(sems.shape[0]):
        part = pl.ds(n * rows, rows)
        copies.append(pltpu.make_async_copy(og_hbm.at[part], og_ref.at[part], sems.at[n]))
        copies[-1].start()
    for copy in copies:
        copy.wait()


def split_body(zh_ref, *refs):
    ins, (keep_ref, give_ref) = refs[:4], refs[4:]
    y = total_of(ins)
    low, high = y[:16], y[16:]
    is_first = zh_ref[0] == 0
    keep_ref[...] = jnp.where(is_first, low, high)
    give_ref[...] = jnp.where(is_first, high, low)


def second_body(total, c_ref, one_ref, two_ref, og_ref, keep_ref, give_ref):
    y = (one_ref[...] + two_ref[...]) / total
    low_half, high_half = y[:8], y[8:]
    is_first = c_ref[0] == 0
    y = jnp.concatenate(
        [
            jnp.where(is_first, low_half, high_half),
            jnp.where(is_first, high_half, low_half),
        ]
    )
    high = y.astype(BF16)
    low = (y - high.astype(F32)).astype(BF16)
    both = jnp.concatenate([high, low])
    chips, _, width = keep_ref.shape
    for i in range(chips):
        columns = og_ref[:, i * width : (i + 1) * width]
        out = jnp.dot(both, columns, preferred_element_type=F32)
        out = out[:16] + out[16:]
        keep_ref[i] = out[:8]
        give_ref[i] = out[8:]


def by_y_body(y_ref, a_ref, b_ref, *outs):
    for k in range(4):
        begin = (y_ref[0] ^ k) * 4
        outs[k][...] = a_ref[pl.ds(begin, 4)] + b_ref[pl.ds(begin, 4)]


def by_zl_body(zl_ref, *refs):
    ins, outs = refs[:4], refs[4:]
    for k in range(4):
        at = zl_ref[0] ^ k
        outs[k][...] = ins[0][at] + ins[1][at] + ins[2][at] + ins[3][at]


def reduce_body(cols, c_ref, *refs):
    ins, (keep_ref, give_ref) = refs[:-2], refs[-2:]
    if len(ins) == 1:
        parts_ref = ins[0]
        done = []
        for zh in range(2):
            plane = parts_ref[4 * zh]
            for zl in range(1, 4):
                plane = plane + parts_ref[4 * zh + zl]
            done.append(plane)
        done = jnp.concatenate(done)
    else:
        done = total_of(ins)
    squares = jnp.sum(jnp.sum(done * done, axis=0, keepdims=True), axis=1, keepdims=True)
    wide = keep_ref.shape[1]
    left = done[:, :wide]
    right = pltpu.roll(done, cols, 1)[:, :wide]
    is_first = c_ref[0] == 0
    lane = lax.broadcasted_iota(jnp.int32, left.shape, 1)
    keep_ref[...] = jnp.where(lane < cols, jnp.where(is_first, left, right), squares)
    give_ref[...] = jnp.where(lane < cols, jnp.where(is_first, right, left), squares)


def pair_body(cols, me_ref, keep_ref, got_ref, *outs):
    keep, got = keep_ref[...], got_ref[...]
    is_first = me_ref[0] == 0
    half = keep.shape[0]
    both = keep + got
    lane = lax.broadcasted_iota(jnp.int32, keep.shape, 1)
    outs[0][:half] = jnp.where(lane < cols, jnp.where(is_first, keep, got), both)
    outs[0][half:] = jnp.where(lane < cols, jnp.where(is_first, got, keep), both)
    if len(outs) == 2:
        line = both[0:1, both.shape[1] - 1 :]
        outs[1][...] = jnp.broadcast_to(line, outs[1].shape)


def last_body(
    steps,
    x_ref,
    squares_ref,
    lines0_ref,
    lines1_ref,
    lines2_ref,
    lines3_ref,
    first_ref,
    second_ref,
    proj_ref,
    weight_ref,
    new_weight_hbm,
    new_first_hbm,
    new_second_hbm,
    rows_ref,
    turned_ref,
    new_weight_ref,
    new_first_ref,
    new_second_ref,
    sems,
):
    for k, ref in zip(ORDER, (lines0_ref, lines1_ref, lines2_ref, lines3_ref)):
        begin = pl.multiple_of((x_ref[0] ^ k) * 32, 32)
        rows_ref[pl.ds(begin, 32), :] = ref[...]
    turned_ref[...] = rows_ref[...].T
    squares = jnp.sum(squares_ref[...], axis=0)[0:1]
    factor = jnp.minimum(jnp.float32(1.0), 1.0 / jnp.sqrt(squares + 1e-12))
    fix_one = 1.0 - 0.9**STEP
    fix_two = 1.0 - 0.999**STEP
    chunk = first_ref.shape[0] // steps
    copies = []
    for i in range(steps):
        here = pl.ds(i * chunk, chunk)
        clipped = factor * turned_ref[here, :]
        new_first = 0.9 * first_ref[here, :] + 0.1 * clipped
        new_second = 0.999 * second_ref[here, :] + 0.001 * clipped * clipped
        new_first_ref[here, :] = new_first
        new_second_ref[here, :] = new_second
        direction = new_first / fix_one / (jnp.sqrt(new_second / fix_two) + 1e-08)
        delta = lax.dot_general(
            direction.astype(BF16),
            proj_ref[...],
            (((1,), (1,)), ((), ())),
            preferred_element_type=F32,
        )
        new_weight_ref[here, :] = weight_ref[here, :].astype(F32) - 0.04 * 0.25 * delta
        for n, (src, dst) in enumerate(
            (
                (new_weight_ref, new_weight_hbm),
                (new_first_ref, new_first_hbm),
                (new_second_ref, new_second_hbm),
            )
        ):
            copies.append(pltpu.make_async_copy(src.at[here], dst.at[here], sems.at[i, n]))
            copies[-1].start()
    for copy in copies:
        copy.wait()


def per_device(acts, out_grads, projector, weight, first_moment, second_moment):
    tokens = acts.shape[1]
    total = float(tokens * 32)
    rows, rank = projector.shape
    columns = out_grads.shape[2]
    cols = first_moment.shape[1]
    width = 2 * cols
    chips = columns // width
    wide = 512
    me_y, me_zl, me_c, me_x, me_zh = [lax.axis_index(name).reshape(1) for name in FINE]

    y = run(
        first_body,
        [(32, tokens)] * 4,
        [SMEM, HBM, HBM],
        (me_x, in_hbm(acts[0]), in_hbm(projector)),
        [
            pltpu.VMEM((tokens, rows), BF16),
            pltpu.VMEM((rows, rank), BF16),
            pltpu.VMEM((rank, tokens), F32),
            pltpu.SemaphoreType.DMA((3,)),
        ],
    )
    y = trade(y, "x")
    keep, give = run(split_body, [(16, tokens)] * 2, [SMEM] + [VMEM] * 4, (me_zh, *y))
    got = swap(give, "zh")
    og = run(
        fetch_body,
        ((tokens, columns), BF16),
        [HBM, HBM],
        (in_hbm(out_grads[0]), keep),
        [pltpu.SemaphoreType.DMA((4,))],
        nbytes=16 << 20,
    )
    keep, give = run(
        functools.partial(second_body, total),
        [(chips, 8, width)] * 2,
        [SMEM] + [VMEM] * 3,
        (me_c, keep, got, og),
        flops=2 * 32 * tokens * columns,
        nbytes=8 << 20,
    )
    parts = run(by_y_body, [(4, 8, width)] * 4, [SMEM, VMEM, VMEM], (me_y, keep, swap(give, "c")))
    parts = trade(parts, "y")
    parts = run(by_zl_body, [(8, width)] * 4, [SMEM] + [VMEM] * 4, (me_zl, *parts))
    parts = trade(parts, "zl", (2, 1, 3))
    pair = functools.partial(pair_body, cols)
    keep, give = run(
        functools.partial(reduce_body, cols),
        [(8, wide)] * 2,
        [SMEM] + [VMEM] * 4,
        (me_c, *parts),
    )
    keep = run(pair, (16, wide), [SMEM, VMEM, VMEM], (me_c, keep, swap(give, "c")))
    line, squares = run(
        pair,
        [(32, wide), (64, 2, 128)],
        [SMEM, VMEM, VMEM],
        (me_zh, keep, swap(keep, "zh")),
    )
    squares = lax.all_to_all(squares, ("y", "zl", "x"), 0, 0, tiled=True)
    lines = trade([line] * 4, "x")

    steps = 4
    outs = [(cols, rows), (cols, rank), (cols, rank)]
    new_weight, new_first, new_second = pl.pallas_call(
        functools.partial(last_body, steps),
        in_specs=[SMEM] + [VMEM] * 9,
        out_specs=(HBM,) * 3,
        out_shape=tuple(jax.ShapeDtypeStruct(shape, F32) for shape in outs),
        scratch_shapes=[
            pltpu.VMEM((rank, wide), F32),
            pltpu.VMEM((wide, rank), F32),
            *[pltpu.VMEM(shape, F32) for shape in outs],
            pltpu.SemaphoreType.DMA((steps, 3)),
        ],
        compiler_params=pltpu.CompilerParams(vmem_limit_bytes=LIMIT),
        cost_estimate=pl.CostEstimate(
            flops=2 * cols * rows * rank, bytes_accessed=4 << 20, transcendentals=0
        ),
    )(me_x, squares, *lines, first_moment.T, second_moment.T, projector, weight.T)
    return (new_weight.T, new_first.T, new_second.T)


def solution(mesh):
    fine = Mesh(mesh.devices.reshape(SIZES), FINE)
    placed = (
        P(DP, None, TENSOR),
        P(DP, None, None),
        P(TENSOR, None),
        P(TENSOR, DP),
        P(None, DP),
        P(None, DP),
    )
    return jax.shard_map(
        per_device,
        mesh=fine,
        in_specs=placed,
        out_specs=(P(TENSOR, DP), P(None, DP), P(None, DP)),
        check_vma=False,
    )
```

```python
import functools

import jax
import jax.numpy as jnp
from jax import lax
from jax.experimental import pallas as pl
from jax.experimental.pallas import tpu as pltpu
from jax.sharding import Mesh
from jax.sharding import PartitionSpec as P

STEP = 10
FINE = ("y", "zl", "c", "x", "zh")
SIZES = (4, 4, 2, 4, 2)
DP = ("y", "zl", "c")
TENSOR = ("x", "zh")
VMEM = pl.BlockSpec(memory_space=pltpu.VMEM)
SMEM = pl.BlockSpec(memory_space=pltpu.SMEM)
HBM = pl.BlockSpec(memory_space=pl.ANY)
LIMIT = 6 << 20
ORDER = (3, 2, 1, 0)
F32 = jnp.float32
BF16 = jnp.bfloat16


def swap(value, axis):
    return lax.ppermute(value, axis, [(0, 1), (1, 0)])


def trade(values, axis, order=(3, 2, 1)):
    return [lax.ppermute(values[k], axis, [(i, i ^ k) for i in range(4)]) for k in order] + [
        values[0]
    ]


def in_hbm(value):
    return pltpu.with_memory_space_constraint(value, pltpu.HBM)


def run(body, outs, specs, args, scratch=(), flops=0, nbytes=1 << 20):
    single = not isinstance(outs, list)
    made = [
        pltpu.VMEM(*(s if isinstance(s[0], tuple) else (s, F32))) for s in ([outs] if single else outs)
    ]
    return pl.pallas_call(
        body,
        in_specs=specs,
        out_shape=made[0] if single else tuple(made),
        out_specs=VMEM if single else tuple(VMEM for _ in made),
        scratch_shapes=list(scratch),
        compiler_params=pltpu.CompilerParams(vmem_limit_bytes=LIMIT),
        cost_estimate=pl.CostEstimate(flops=flops, bytes_accessed=nbytes, transcendentals=0),
    )(*args)


def total_of(refs):
    total = refs[0][...]
    for ref in refs[1:]:
        total = total + ref[...]
    return total


def first_body(x_ref, acts_hbm, proj_hbm, *rest):
    outs, (acts_ref, proj_ref, turned_ref, sems) = rest[:-4], rest[-4:]
    one = pltpu.make_async_copy(acts_hbm, acts_ref, sems.at[0])
    two = pltpu.make_async_copy(proj_hbm, proj_ref, sems.at[1])
    two.start()
    one.start()
    two.wait()
    one.wait()
    y = jnp.dot(acts_ref[...], proj_ref[...], preferred_element_type=F32)
    turned_ref[...] = y.T
    for k in range(4):
        begin = pl.multiple_of((x_ref[0] ^ k) * 32, 32)
        outs[k][...] = turned_ref[pl.ds(begin, 32), :]


def fetch_body(og_hbm, after_ref, og_ref, sems):
    rows = og_hbm.shape[0] // sems.shape[0]
    copies = []
    for n in range(sems.shape[0]):
        part = pl.ds(n * rows, rows)
        copies.append(pltpu.make_async_copy(og_hbm.at[part], og_ref.at[part], sems.at[n]))
        copies[-1].start()
    for copy in copies:
        copy.wait()


def split_body(zh_ref, *refs):
    ins, (keep_ref, give_ref) = refs[:4], refs[4:]
    y = total_of(ins)
    low, high = y[:16], y[16:]
    is_first = zh_ref[0] == 0
    keep_ref[...] = jnp.where(is_first, low, high)
    give_ref[...] = jnp.where(is_first, high, low)


def second_body(total, c_ref, one_ref, two_ref, og_ref, keep_ref, give_ref):
    y = (one_ref[...] + two_ref[...]) / total
    low_half, high_half = y[:8], y[8:]
    is_first = c_ref[0] == 0
    y = jnp.concatenate(
        [
            jnp.where(is_first, low_half, high_half),
            jnp.where(is_first, high_half, low_half),
        ]
    )
    high = y.astype(BF16)
    low = (y - high.astype(F32)).astype(BF16)
    both = jnp.concatenate([high, low])
    chips, _, width = keep_ref.shape
    for i in range(chips):
        columns = og_ref[:, i * width : (i + 1) * width]
        out = jnp.dot(both, columns, preferred_element_type=F32)
        out = out[:16] + out[16:]
        keep_ref[i] = out[:8]
        give_ref[i] = out[8:]


def by_y_body(y_ref, a_ref, b_ref, *outs):
    for k in range(4):
        begin = (y_ref[0] ^ k) * 4
        outs[k][...] = a_ref[pl.ds(begin, 4)] + b_ref[pl.ds(begin, 4)]


def by_zl_body(zl_ref, *refs):
    ins, outs = refs[:4], refs[4:]
    for k in range(4):
        at = zl_ref[0] ^ k
        outs[k][...] = ins[0][at] + ins[1][at] + ins[2][at] + ins[3][at]


def reduce_body(cols, c_ref, *refs):
    ins, (keep_ref, give_ref) = refs[:-2], refs[-2:]
    if len(ins) == 1:
        parts_ref = ins[0]
        done = []
        for zh in range(2):
            plane = parts_ref[4 * zh]
            for zl in range(1, 4):
                plane = plane + parts_ref[4 * zh + zl]
            done.append(plane)
        done = jnp.concatenate(done)
    else:
        done = total_of(ins)
    squares = jnp.sum(jnp.sum(done * done, axis=0, keepdims=True), axis=1, keepdims=True)
    wide = keep_ref.shape[1]
    left = done[:, :wide]
    right = pltpu.roll(done, cols, 1)[:, :wide]
    is_first = c_ref[0] == 0
    lane = lax.broadcasted_iota(jnp.int32, left.shape, 1)
    keep_ref[...] = jnp.where(lane < cols, jnp.where(is_first, left, right), squares)
    give_ref[...] = jnp.where(lane < cols, jnp.where(is_first, right, left), squares)


def pair_body(cols, me_ref, keep_ref, got_ref, *outs):
    keep, got = keep_ref[...], got_ref[...]
    is_first = me_ref[0] == 0
    half = keep.shape[0]
    both = keep + got
    lane = lax.broadcasted_iota(jnp.int32, keep.shape, 1)
    outs[0][:half] = jnp.where(lane < cols, jnp.where(is_first, keep, got), both)
    outs[0][half:] = jnp.where(lane < cols, jnp.where(is_first, got, keep), both)
    if len(outs) == 2:
        line = both[0:1, both.shape[1] - 1 :]
        outs[1][...] = jnp.broadcast_to(line, outs[1].shape)


def last_body(
    steps,
    x_ref,
    squares_ref,
    lines0_ref,
    lines1_ref,
    lines2_ref,
    lines3_ref,
    first_ref,
    second_ref,
    proj_ref,
    weight_ref,
    new_weight_hbm,
    new_first_hbm,
    new_second_hbm,
    rows_ref,
    turned_ref,
    new_weight_ref,
    new_first_ref,
    new_second_ref,
    sems,
):
    for k, ref in zip(ORDER, (lines0_ref, lines1_ref, lines2_ref, lines3_ref)):
        begin = pl.multiple_of((x_ref[0] ^ k) * 32, 32)
        rows_ref[pl.ds(begin, 32), :] = ref[...]
    turned_ref[...] = rows_ref[...].T
    squares = jnp.sum(squares_ref[...], axis=0)[0:1]
    factor = jnp.minimum(jnp.float32(1.0), 1.0 / jnp.sqrt(squares + 1e-12))
    fix_one = 1.0 - 0.9**STEP
    fix_two = 1.0 - 0.999**STEP
    chunk = first_ref.shape[0] // steps
    copies = []
    for i in range(steps):
        here = pl.ds(i * chunk, chunk)
        clipped = factor * turned_ref[here, :]
        new_first = 0.9 * first_ref[here, :] + 0.1 * clipped
        new_second = 0.999 * second_ref[here, :] + 0.001 * clipped * clipped
        new_first_ref[here, :] = new_first
        new_second_ref[here, :] = new_second
        direction = new_first / fix_one / (jnp.sqrt(new_second / fix_two) + 1e-08)
        delta = lax.dot_general(
            direction.astype(BF16),
            proj_ref[...],
            (((1,), (1,)), ((), ())),
            preferred_element_type=F32,
        )
        new_weight_ref[here, :] = weight_ref[here, :].astype(F32) - 0.04 * 0.25 * delta
        for n, (src, dst) in enumerate(
            (
                (new_weight_ref, new_weight_hbm),
                (new_first_ref, new_first_hbm),
                (new_second_ref, new_second_hbm),
            )
        ):
            copies.append(pltpu.make_async_copy(src.at[here], dst.at[here], sems.at[i, n]))
            copies[-1].start()
    for copy in copies:
        copy.wait()


def per_device(acts, out_grads, projector, weight, first_moment, second_moment):
    tokens = acts.shape[1]
    total = float(tokens * 32)
    rows, rank = projector.shape
    columns = out_grads.shape[2]
    cols = first_moment.shape[1]
    width = 2 * cols
    chips = columns // width
    wide = 512
    me_y, me_zl, me_c, me_x, me_zh = [lax.axis_index(name).reshape(1) for name in FINE]

    y = run(
        first_body,
        [(32, tokens)] * 4,
        [SMEM, HBM, HBM],
        (me_x, in_hbm(acts[0]), in_hbm(projector)),
        [
            pltpu.VMEM((tokens, rows), BF16),
            pltpu.VMEM((rows, rank), BF16),
            pltpu.VMEM((rank, tokens), F32),
            pltpu.SemaphoreType.DMA((2,)),
        ],
    )
    y = trade(y, "x")
    keep, give = run(split_body, [(16, tokens)] * 2, [SMEM] + [VMEM] * 4, (me_zh, *y))
    got = swap(give, "zh")
    og = run(
        fetch_body,
        ((tokens, columns), BF16),
        [HBM, HBM],
        (in_hbm(out_grads[0]), keep),
        [pltpu.SemaphoreType.DMA((4,))],
        nbytes=16 << 20,
    )
    keep, give = run(
        functools.partial(second_body, total),
        [(chips, 8, width)] * 2,
        [SMEM] + [VMEM] * 3,
        (me_c, keep, got, og),
        flops=2 * 32 * tokens * columns,
        nbytes=8 << 20,
    )
    parts = run(by_y_body, [(4, 8, width)] * 4, [SMEM, VMEM, VMEM], (me_y, keep, swap(give, "c")))
    parts = trade(parts, "y")
    parts = run(by_zl_body, [(8, width)] * 4, [SMEM] + [VMEM] * 4, (me_zl, *parts))
    parts = trade(parts, "zl", (2, 1, 3))
    pair = functools.partial(pair_body, cols)
    keep, give = run(
        functools.partial(reduce_body, cols),
        [(8, wide)] * 2,
        [SMEM] + [VMEM] * 4,
        (me_c, *parts),
    )
    keep = run(pair, (16, wide), [SMEM, VMEM, VMEM], (me_c, keep, swap(give, "c")))
    line, squares = run(
        pair,
        [(32, wide), (64, 2, 128)],
        [SMEM, VMEM, VMEM],
        (me_zh, keep, swap(keep, "zh")),
    )
    squares = lax.all_to_all(squares, ("y", "zl", "x"), 0, 0, tiled=True)
    lines = trade([line] * 4, "x")

    steps = 4
    outs = [(cols, rows), (cols, rank), (cols, rank)]
    new_weight, new_first, new_second = pl.pallas_call(
        functools.partial(last_body, steps),
        in_specs=[SMEM] + [VMEM] * 9,
        out_specs=(HBM,) * 3,
        out_shape=tuple(jax.ShapeDtypeStruct(shape, F32) for shape in outs),
        scratch_shapes=[
            pltpu.VMEM((rank, wide), F32),
            pltpu.VMEM((wide, rank), F32),
            *[pltpu.VMEM(shape, F32) for shape in outs],
            pltpu.SemaphoreType.DMA((steps, 3)),
        ],
        compiler_params=pltpu.CompilerParams(vmem_limit_bytes=LIMIT),
        cost_estimate=pl.CostEstimate(
            flops=2 * cols * rows * rank, bytes_accessed=4 << 20, transcendentals=0
        ),
    )(me_x, squares, *lines, first_moment.T, second_moment.T, projector, weight.T)
    return (new_weight.T, new_first.T, new_second.T)


def solution(mesh):
    fine = Mesh(mesh.devices.reshape(SIZES), FINE)
    placed = (
        P(DP, None, TENSOR),
        P(DP, None, None),
        P(TENSOR, None),
        P(TENSOR, DP),
        P(None, DP),
        P(None, DP),
    )
    return jax.shard_map(
        per_device,
        mesh=fine,
        in_specs=placed,
        out_specs=(P(TENSOR, DP), P(None, DP), P(None, DP)),
        check_vma=False,
    )
```
